32 devices in a mesh: groups: 2 (over x), section: 2 (over core), zero: 8 (over z, y).
Axes of the slice: x: 2, y: 2, z: 4, core: 2. Of those that a mesh axis runs over, the one named last changes fastest.
Arguments:
- inputs: bfloat16 [2048, 8192], P(('groups', 'zero')), parts along dimension 0, may hold values from -6 to 6
- cotangent: bfloat16 [2048, 8192], P(('groups', 'zero')), parts along dimension 0, may hold values from -6 to 6
- weights: bfloat16 [2, 3, 128, 2, 4096], P('section', None, 'zero'), may hold values from -0.75 to 0.75
- keep: int32 [2, 3, 128, 2], P('section', None, 'zero'), may hold values from 0 to 1, as said below
- columns: int32 [2, 3, 128, 2], P('section'), may hold values from 0 to 171, as said below
Outputs:
- outputs: bfloat16 [2, 2048, 8192], P('section', ('groups', 'zero')), parts along dimension 1
- grad_input: bfloat16 [2, 2048, 8192], P('section', ('groups', 'zero')), parts along dimension 1
- grad_weight: float32 [2, 3, 256, 2, 4096], P('section', None, ('groups', 'zero')), parts along dimension 2
The draws below stay inside these ranges and needn't reach their ends.
There are 2 independent parts, one for each index of `groups`. The reference program is written for one: setup_inputs(seed, part) draws one part's arguments, and reference() takes and returns one part's arrays. A program takes and returns all parts, laid end to end along the dimension named above; an argument that names none is the same for every part. Nothing has to cross between parts.
Inputs may be any that keep to these rules, and one draw needn't show every extreme that they name: In every layer and every matrix the 32 slots of the rows held by one device of zero (16 block rows) keep between 8 and 32, and the rows of some device keep all 32. The 2 columns of one block row of one matrix are different.
All inputs are finite; a program needn't handle non-finite values.
Results may differ from the reference program's by a relative error of at most 0.01.
Values may be sent and summed in bfloat16 or wider, within the bound.
A program may use at most 192 MiB of HBM per device.

```python
import math
import jax
import jax.numpy as jnp
from jax import lax

D = 8192
BLK = 64
KPR = 2
TOK_DEV = 128
SECTIONS = 2
TOKENS = 1024
NBR = 128
NBC = 172
RPS = 16
CAP = 32
LOW = 8
N_ZERO = 8


def draw_keep(key, part):
    shards = NBR // RPS
    key_count, key_full, key_rank = jax.random.split(key, 3)
    counts = jax.random.randint(key_count, (SECTIONS, 3, shards), LOW, CAP + 1)
    fullest = jax.random.randint(key_full, (SECTIONS, 3), 0, shards)
    counts = jnp.where(jnp.arange(shards)[None, None, :] == fullest[:, :, None], CAP, counts)
    rank_keys = jax.random.split(key_rank, SECTIONS * 3 * shards)
    ranks = jax.vmap(lambda single: jax.random.permutation(single, CAP))(rank_keys)
    ranks = ranks.reshape(SECTIONS, 3, shards, CAP)
    kept = (ranks < counts[:, :, :, None]).astype(jnp.int32)
    return kept.reshape(SECTIONS, 3, NBR, KPR)


def draw_columns(key, part):
    row_keys = jax.random.split(jax.random.fold_in(key, 7), SECTIONS * 3 * NBR)
    orders = jax.vmap(lambda single: jax.random.permutation(single, NBC))(row_keys)
    return orders[:, :KPR].astype(jnp.int32).reshape(SECTIONS, 3, NBR, KPR)


def with_spikes(result, own_key, source, target, shards_of, factor):
    def block_of(dim):
        return (jnp.arange(result.shape[dim]) // (result.shape[dim] // shards_of)).reshape((-1,) + (1,) * (result.ndim - 1 - dim))

    first = jax.random.permutation(own_key, shards_of)[block_of(target)]
    other_side = (block_of(target) + shards_of // 2) % shards_of
    return jnp.where((block_of(source) == first) | (block_of(source) == other_side), factor * result, result)


def block_scale(key, shape, cuts, least, top_value):
    level = 1.0
    for dim, blocks in cuts:
        heights = jax.random.uniform(jax.random.fold_in(jax.random.fold_in(key, 6), dim), (blocks,), jnp.float32, least / len(cuts), top_value / len(cuts))
        level = level * jnp.repeat(jnp.exp(heights), shape[dim] // blocks).reshape((-1,) + (1,) * (len(shape) - 1 - dim))
    return level


def scatter_about(rng, extent, deviation, limit, cuts=(), held_as=jnp.bfloat16):
    result = deviation * jax.random.normal(rng, extent, jnp.float32)
    if cuts:
        result = result * block_scale(rng, extent, cuts, -0.22, 0.18)
    return jnp.clip(result, -limit, limit).astype(held_as)


def heavy_noise(rng, shape, width, bound, cuts, heavy, kind=jnp.bfloat16):
    array = width * jax.random.normal(rng, shape, jnp.float32)
    if cuts:
        array = array * block_scale(rng, shape, cuts, -0.22, 0.18)
    return jnp.clip(with_spikes(array, jax.random.fold_in(rng, 3), *heavy), -bound, bound).astype(kind)


def setup_inputs(seed: int = 0, part: int = 0) -> dict:
    streams_of = jax.random.split(jax.random.key(seed), 6)
    part_splits = jax.random.split(jax.random.fold_in(streams_of[5], part), 6)
    return {
        "inputs": heavy_noise(part_splits[0], (TOKENS, D), 1.0, 6.0, ((0, 8),), (0, 1, 8, 2.0)),
        "cotangent": heavy_noise(part_splits[1], (TOKENS, D), 1.0, 6.0, ((0, 8),), (0, 1, 8, 2.0)),
        "weights": scatter_about(streams_of[2], (SECTIONS, 3, NBR, KPR, BLK * BLK), BLK ** -0.5, 0.75, ((0, 2), (2, 8))),
        "keep": draw_keep(jax.random.fold_in(streams_of[5], 71), part),
        "columns": draw_columns(jax.random.fold_in(streams_of[5], 71), part),
    }


epsilon = 1e-05

def spread_in(rows_in, block_set, column_set):
    count = rows_in.shape[0]
    row_blocks, slots = column_set.shape
    shaped_in = rows_in.reshape(count, row_blocks, BLK).astype(jnp.float32)
    shaped_w = block_set.reshape(row_blocks, slots, BLK, BLK).astype(jnp.float32)
    parts = jnp.einsum('trb,rkbe->trke', shaped_in, shaped_w, precision=lax.Precision.HIGHEST)
    placed = jnp.zeros((count, NBC, BLK), jnp.float32)
    placed = placed.at[:, column_set.reshape(-1)].add(parts.reshape(count, row_blocks * slots, BLK))
    return placed.reshape(count, NBC * BLK)

def pick_columns(hidden_in, column_set):
    count = hidden_in.shape[0]
    row_blocks, slots = column_set.shape
    picked = hidden_in.reshape(count, NBC, BLK)[:, column_set.reshape(-1)]
    return picked.reshape(count, row_blocks, slots, BLK)

def gather_out(hidden_in, block_set, column_set):
    count = hidden_in.shape[0]
    row_blocks, slots = column_set.shape
    picked = pick_columns(hidden_in, column_set).astype(jnp.float32)
    shaped_w = block_set.reshape(row_blocks, slots, BLK, BLK).astype(jnp.float32)
    out = jnp.einsum('trkj,rkij->tri', picked, shaped_w, precision=lax.Precision.HIGHEST)
    return out.reshape(count, row_blocks * BLK)

def block_terms(left, right, column_set):
    count = left.shape[0]
    row_blocks, slots = column_set.shape
    rows_in = left.reshape(count, row_blocks, BLK).astype(jnp.float32)
    picked = pick_columns(right, column_set).astype(jnp.float32)
    terms = jnp.einsum('tri,trkj->rkij', rows_in, picked, precision=lax.Precision.HIGHEST)
    return terms.reshape(row_blocks, slots, BLK * BLK)

def layer_front(layer_in, blocks, column_sets):
    widened = layer_in.astype(jnp.float32)
    reciprocal = lax.rsqrt(lax.optimization_barrier(jnp.mean(widened * widened, axis=-1, keepdims=True)) + epsilon)
    scaled = widened * reciprocal
    normed = scaled.astype(jnp.bfloat16)
    pre_gate = spread_in(normed, blocks[0], column_sets[0])
    pre_up = spread_in(normed, blocks[1], column_sets[1])
    return (widened, reciprocal, scaled, normed, pre_gate, pre_up)

def forward_layer(layer_in, blocks, column_sets):
    widened, reciprocal, scaled, normed, pre_gate, pre_up = layer_front(layer_in, blocks, column_sets)
    hidden = (jax.nn.silu(pre_gate) * pre_up).astype(jnp.bfloat16)
    returned = gather_out(hidden, blocks[2], column_sets[2])
    return (widened + returned).astype(jnp.bfloat16)

def backward_layer(layer_in, upstream, blocks, column_sets):
    widened, reciprocal, scaled, normed, pre_gate, pre_up = layer_front(layer_in, blocks, column_sets)
    logistic = jax.nn.sigmoid(pre_gate)
    silu_gate = pre_gate * logistic
    hidden = (silu_gate * pre_up).astype(jnp.bfloat16)
    grad_hidden = spread_in(upstream, blocks[2], column_sets[2])
    grad_gate = (grad_hidden * pre_up * logistic * (1.0 + pre_gate * (1.0 - logistic))).astype(jnp.bfloat16)
    grad_up = (grad_hidden * silu_gate).astype(jnp.bfloat16)
    grad_normed = gather_out(grad_gate, blocks[0], column_sets[0]) + gather_out(grad_up, blocks[1], column_sets[1])
    inner = lax.optimization_barrier(jnp.mean(grad_normed * scaled, axis=-1, keepdims=True))
    grad_in = (upstream.astype(jnp.float32) + reciprocal * (grad_normed - scaled * inner)).astype(jnp.bfloat16)
    return (grad_in, (normed, grad_gate, grad_up, upstream, hidden))

def token_sums(pieces, column_sets):
    shaped = tuple((p.reshape(N_ZERO, TOK_DEV, p.shape[1]) for p in pieces))

    def add_block(total, items):
        term = jnp.stack([block_terms(items[0], items[1], column_sets[0]), block_terms(items[0], items[2], column_sets[1]), block_terms(items[3], items[4], column_sets[2])])
        rounded = lax.optimization_barrier(term.astype(jnp.bfloat16)).astype(jnp.float32)
        return (total + rounded, None)
    start = jnp.zeros((3, NBR, KPR, BLK * BLK), jnp.float32)
    total, unused = lax.scan(add_block, start, shaped)
    return total

def reference(inputs, cotangent, weights, keep, columns):
    norm_factor = 1.0 / math.sqrt(TOKENS)
    masked = (weights * keep[..., None].astype(weights.dtype)).astype(jnp.bfloat16)
    current = inputs
    saved_in = []
    layer_outs = []
    for layer in range(SECTIONS):
        saved_in.append(current)
        current = forward_layer(current, masked[layer], columns[layer])
        layer_outs.append(current)
    upstream = cotangent
    grads_in = [None] * SECTIONS
    grads_w = [None] * SECTIONS
    for layer in range(SECTIONS - 1, -1, -1):
        upstream, pieces = backward_layer(saved_in[layer], upstream, masked[layer], columns[layer])
        grads_in[layer] = upstream
        grads_w[layer] = token_sums(pieces, columns[layer]) * keep[layer][..., None].astype(jnp.float32) * norm_factor
    return (jnp.stack(layer_outs), jnp.stack(grads_in), jnp.stack(grads_w))
```

```python
import math

import jax
import jax.numpy as jnp
from jax import lax
from jax.experimental import pallas as pl
from jax.experimental.pallas import tpu as pltpu
from jax.sharding import PartitionSpec as P

FF = 11008
BLK = 64
NBC = FF // BLK
BF = jnp.bfloat16
F32 = jnp.float32
epsilon = 1e-05

TN = (((0,), (0,)), ((), ()))
NT = (((1,), (1,)), ((), ()))


def dot(a, b, dims=(((1,), (0,)), ((), ()))):
    return lax.dot_general(a, b, dims, preferred_element_type=F32)


def total_rows(acc):
    return jnp.sum(acc, axis=0, keepdims=True)


def fold(value):
    return jnp.sum(value.reshape(-1, 8, value.shape[-1]), axis=0)


def looped(count, unroll, body):
    def step(i, carry):
        for k in range(unroll):
            body(i * unroll + k)
        return carry

    lax.fori_loop(0, count // unroll, step, 0)


def norm_scale(a_ref):
    rows, blk, tokens = a_ref.shape

    def add(i, acc):
        for k in range(4):
            v = a_ref[i * 4 + k].astype(F32)
            acc = acc + fold(v * v)
        return acc

    acc = lax.fori_loop(0, rows // 4, add, jnp.zeros((8, tokens), F32))
    return lax.rsqrt(total_rows(acc) / (rows * blk) + epsilon)


def column(cols, m, r, k, rows):
    return cols[(m * rows + r) * 2 + k]


def clear(*refs):
    def body(c):
        for ref in refs:
            ref[c] = jnp.zeros(ref.shape[1:], ref.dtype)

    looped(NBC, 4, body)


def spread(cols, m, rows, r, w, x, out):
    res = dot(w, x, TN)
    for k in range(2):
        c = column(cols, m, r, k, rows)
        out[c] += res[k * BLK : (k + 1) * BLK]


def pick(cols, m, rows, r, src):
    return [src[column(cols, m, r, k, rows)] for k in range(2)]


def forward_into(cols, a_ref, w_ref, out_ref, xn, pg, pu, hid, fa=None, fb=None):
    rows = a_ref.shape[0]
    recip = norm_scale(a_ref)

    def normed(r):
        xn[r] = (a_ref[r].astype(F32) * recip).astype(BF)

    looped(rows, 4, normed)
    clear(pg, pu)

    def up(r):
        x = xn[r]
        spread(cols, 0, rows, r, w_ref[0, r], x, pg)
        spread(cols, 1, rows, r, w_ref[1, r], x, pu)

    looped(rows, 4, up)

    def act(c):
        g = pg[c]
        u = pu[c]
        s = 1.0 / (1.0 + jnp.exp(-g))
        silu = g * s
        hid[c] = (silu * u).astype(BF)
        if fa is not None:
            fa[c] = (u * s * (1.0 + g * (1.0 - s))).astype(BF)
            fb[c] = silu.astype(BF)

    looped(NBC, 2, act)

    def down(r):
        o = dot(w_ref[2, r], jnp.concatenate(pick(cols, 2, rows, r, hid), axis=0))
        out_ref[r] = (a_ref[r].astype(F32) + o).astype(BF)

    looped(rows, 4, down)


def backward_into(cols, a_ref, g_ref, w_ref, fa, fb, gh, gg, gu, gn, gin_ref, between=None):
    rows, blk, tokens = a_ref.shape
    recip = norm_scale(a_ref)
    clear(gh)
    looped(rows, 4, lambda r: spread(cols, 2, rows, r, w_ref[2, r], g_ref[r], gh))

    def act(c):
        v = gh[c]
        gg[c] = (v * fa[c].astype(F32)).astype(BF)
        gu[c] = (v * fb[c].astype(F32)).astype(BF)

    looped(NBC, 2, act)

    def back(i, acc):
        for k in range(4):
            r = i * 4 + k
            right = pick(cols, 0, rows, r, gg) + pick(cols, 1, rows, r, gu)
            left = jnp.concatenate([w_ref[0, r], w_ref[1, r]], axis=1)
            v = dot(left, jnp.concatenate(right, axis=0))
            gn[r] = v
            acc = acc + fold(v * (a_ref[r].astype(F32) * recip))
        return acc

    acc = lax.fori_loop(0, rows // 4, back, jnp.zeros((8, tokens), F32))
    inner = total_rows(acc) / (rows * blk)

    def finish(r):
        q = a_ref[r].astype(F32) * recip
        gin_ref[r] = (g_ref[r].astype(F32) + recip * (gn[r] - q * inner)).astype(BF)

    looped(rows, 4, finish)


def first_kernel(cols, a_ref, w_ref, out_ref, xn, pg, pu, hid):
    forward_into(cols, a_ref, w_ref, out_ref, xn, pg, pu, hid)


def middle_kernel(cols, a_ref, g_ref, w_ref, out_ref, gin_ref, fa, fb, hid, xn, pg, pu, gg, gu, gn):
    forward_into(cols, a_ref, w_ref, out_ref, xn, pg, pu, hid, fa, fb)
    backward_into(cols, a_ref, g_ref, w_ref, fa, fb, pg, gg, gu, gn, gin_ref)


def last_kernel(cols, a_ref, g_ref, w_ref, fa, fb, hid, gin_ref, wg_ref, gh, gg, gu, gn):
    rows = a_ref.shape[0]
    backward_into(cols, a_ref, g_ref, w_ref, fa, fb, gh, gg, gu, gn, gin_ref)
    recip = norm_scale(a_ref)

    def terms(r):
        x = (a_ref[r].astype(F32) * recip).astype(BF)
        right = pick(cols, 0, rows, r, gg) + pick(cols, 1, rows, r, gu)
        t = dot(x, jnp.concatenate(right, axis=0), NT).astype(BF)
        wg_ref[0, r] = t[:, : 2 * BLK]
        wg_ref[1, r] = t[:, 2 * BLK :]
        t = dot(g_ref[r], jnp.concatenate(pick(cols, 2, rows, r, hid), axis=0), NT)
        wg_ref[2, r] = t.astype(BF)

    looped(rows, 4, terms)


def call(kernel, cols, arrays, outs, scratch):
    vmem = pl.BlockSpec(memory_space=pltpu.VMEM)
    return pl.pallas_call(
        kernel,
        out_shape=[jax.ShapeDtypeStruct(s, d) for s, d in outs],
        in_specs=[pl.BlockSpec(memory_space=pltpu.SMEM)] + [vmem] * len(arrays),
        out_specs=[vmem] * len(outs),
        scratch_shapes=[pltpu.VMEM(s, d) for s, d in scratch],
        compiler_params=pltpu.CompilerParams(vmem_limit_bytes=58 * 2**20),
    )(cols, *arrays)


def shards(inputs, cotangent, weights, keep, columns):
    sections = lax.axis_size("section")
    section_id = lax.axis_index("section")
    tokens, width = inputs.shape
    rows = width // BLK
    norm_factor = 1.0 / math.sqrt(tokens * lax.axis_size("zero"))
    own_keep = keep[0]
    own_rows = own_keep.shape[1]
    masked = weights[0] * own_keep[..., None].astype(BF)
    own = masked.reshape(3, own_rows, 2, BLK, BLK).transpose(0, 1, 3, 2, 4)
    own = own.reshape(3, own_rows, BLK, 2 * BLK)
    mats = lax.all_gather(own, "zero", axis=1, tiled=True)
    cols = columns[0].reshape(-1)
    tall = (rows, BLK, tokens)
    wide = (NBC, BLK, tokens)
    start = inputs.T.reshape(tall)
    cot = cotangent.T.reshape(tall)
    current = start
    for tick in range(1, sections):
        (out,) = call(
            first_kernel, cols, (current, mats), [(tall, BF)],
            [(tall, BF), (wide, F32), (wide, F32), (wide, BF)],
        )
        moved = lax.ppermute(out, "section", [(i, i + 1) for i in range(sections - 1)])
        current = jnp.where(section_id == 0, start, moved)
    out, gin, fa, fb, hid = call(
        middle_kernel, cols, (current, cot, mats),
        [(tall, BF), (tall, BF), (wide, BF), (wide, BF), (wide, BF)],
        [(tall, BF), (wide, F32), (wide, F32), (wide, BF), (wide, BF), (tall, F32)],
    )
    for tick in range(1, sections):
        moved = lax.ppermute(gin, "section", [(i + 1, i) for i in range(sections - 1)])
        upstream = jnp.where(section_id == sections - 1, cot, moved)
        gin, terms = call(
            last_kernel, cols, (current, upstream, mats, fa, fb, hid),
            [(tall, BF), ((3, rows, BLK, 2 * BLK), BF)],
            [(wide, F32), (wide, BF), (wide, BF), (tall, F32)],
        )
    summed = lax.psum_scatter(terms, "zero", scatter_dimension=1, tiled=True).astype(F32)
    grad = summed.reshape(3, own_rows, BLK, 2, BLK).transpose(0, 1, 3, 2, 4)
    grad = grad.reshape(3, own_rows, 2, BLK * BLK)
    grad = grad * own_keep[..., None].astype(F32) * norm_factor
    flat = (width, tokens)
    return (out.reshape(flat).T[None], gin.reshape(flat).T[None], grad[None])


def solution(mesh):
    return jax.shard_map(
        shards,
        mesh=mesh,
        in_specs=(
            P(("groups", "zero"), None),
            P(("groups", "zero"), None),
            P("section", None, "zero", None, None),
            P("section", None, "zero", None),
            P("section", None, None, None),
        ),
        out_specs=(
            P("section", ("groups", "zero"), None),
            P("section", ("groups", "zero"), None),
            P("section", None, ("groups", "zero"), None, None),
        ),
        check_vma=False,
    )
```

```python
import math

import jax
import jax.numpy as jnp
from jax import lax
from jax.experimental import pallas as pl
from jax.experimental.pallas import tpu as pltpu
from jax.sharding import PartitionSpec as P

FF = 11008
BLK = 64
NBC = FF // BLK
BF = jnp.bfloat16
F32 = jnp.float32
epsilon = 1e-05

TN = (((0,), (0,)), ((), ()))
NT = (((1,), (1,)), ((), ()))


def dot(a, b, dims=(((1,), (0,)), ((), ()))):
    return lax.dot_general(a, b, dims, preferred_element_type=F32)


def total_rows(acc):
    return jnp.sum(acc, axis=0, keepdims=True)


def fold(value):
    return jnp.sum(value.reshape(-1, 8, value.shape[-1]), axis=0)


def looped(count, unroll, body):
    def step(i, carry):
        for k in range(unroll):
            body(i * unroll + k)
        return carry

    lax.fori_loop(0, count // unroll, step, 0)


def norm_scale(a_ref):
    rows, blk, tokens = a_ref.shape

    def add(i, acc):
        for k in range(4):
            v = a_ref[i * 4 + k].astype(F32)
            acc = acc + fold(v * v)
        return acc

    acc = lax.fori_loop(0, rows // 4, add, jnp.zeros((8, tokens), F32))
    return lax.rsqrt(total_rows(acc) / (rows * blk) + epsilon)


def column(cols, m, r, k, rows):
    return cols[(m * rows + r) * 2 + k]


def clear(*refs):
    def body(c):
        for ref in refs:
            ref[c] = jnp.zeros(ref.shape[1:], ref.dtype)

    looped(NBC, 4, body)


def spread(cols, m, rows, r, w, x, out):
    res = dot(w, x, TN)
    for k in range(2):
        c = column(cols, m, r, k, rows)
        out[c] += res[k * BLK : (k + 1) * BLK]


def pick(cols, m, rows, r, src):
    return [src[column(cols, m, r, k, rows)] for k in range(2)]


def forward_into(cols, a_ref, w_ref, out_ref, xn, pg, pu, hid, fa=None, fb=None):
    rows = a_ref.shape[0]
    recip = norm_scale(a_ref)

    def normed(r):
        xn[r] = (a_ref[r].astype(F32) * recip).astype(BF)

    looped(rows, 4, normed)
    clear(pg, pu)

    def up(r):
        x = xn[r]
        spread(cols, 0, rows, r, w_ref[0, r], x, pg)
        spread(cols, 1, rows, r, w_ref[1, r], x, pu)

    looped(rows, 4, up)

    def act(c):
        g = pg[c]
        u = pu[c]
        s = 1.0 / (1.0 + jnp.exp(-g))
        silu = g * s
        hid[c] = (silu * u).astype(BF)
        if fa is not None:
            fa[c] = (u * s * (1.0 + g * (1.0 - s))).astype(BF)
            fb[c] = silu.astype(BF)

    looped(NBC, 2, act)

    def down(r):
        o = dot(w_ref[2, r], jnp.concatenate(pick(cols, 2, rows, r, hid), axis=0))
        out_ref[r] = (a_ref[r].astype(F32) + o).astype(BF)

    looped(rows, 4, down)


def backward_into(cols, a_ref, g_ref, w_ref, fa, fb, gh, gg, gu, gn, gin_ref, between=None):
    rows, blk, tokens = a_ref.shape
    recip = norm_scale(a_ref)
    clear(gh)
    looped(rows, 4, lambda r: spread(cols, 2, rows, r, w_ref[2, r], g_ref[r], gh))

    def act(c):
        v = gh[c]
        gg[c] = (v * fa[c].astype(F32)).astype(BF)
        gu[c] = (v * fb[c].astype(F32)).astype(BF)

    looped(NBC, 2, act)

    def back(i, acc):
        for k in range(4):
            r = i * 4 + k
            right = pick(cols, 0, rows, r, gg) + pick(cols, 1, rows, r, gu)
            left = jnp.concatenate([w_ref[0, r], w_ref[1, r]], axis=1)
            v = dot(left, jnp.concatenate(right, axis=0))
            gn[r] = v
            acc = acc + fold(v * (a_ref[r].astype(F32) * recip))
        return acc

    acc = lax.fori_loop(0, rows // 4, back, jnp.zeros((8, tokens), F32))
    inner = total_rows(acc) / (rows * blk)

    def finish(r):
        q = a_ref[r].astype(F32) * recip
        gin_ref[r] = (g_ref[r].astype(F32) + recip * (gn[r] - q * inner)).astype(BF)

    looped(rows, 4, finish)


def first_kernel(cols, sec, a_ref, w_ref, out_ref, xn, pg, pu, hid):
    @pl.when(sec[0] < sec[1] - 1)
    def _():
        forward_into(cols, a_ref, w_ref, out_ref, xn, pg, pu, hid)


def middle_kernel(cols, sec, a_ref, g_ref, w_ref, out_ref, gin_ref, fa, fb, hid, xn, pg, pu, ga, gb, gn):
    forward_into(cols, a_ref, w_ref, out_ref, xn, pg, pu, hid, fa, fb)

    @pl.when(sec[0] == sec[1] - 1)
    def _():
        backward_into(cols, a_ref, g_ref, w_ref, fa, fb, pg, ga, gb, gn, gin_ref)

        def keep_grads(c):
            fa[c] = ga[c]
            fb[c] = gb[c]

        looped(NBC, 4, keep_grads)


def terms_into(cols, a_ref, g_ref, gg, gu, hid, wg_ref):
    rows = a_ref.shape[0]
    recip = norm_scale(a_ref)

    def terms(r):
        x = (a_ref[r].astype(F32) * recip).astype(BF)
        right = pick(cols, 0, rows, r, gg) + pick(cols, 1, rows, r, gu)
        t = dot(x, jnp.concatenate(right, axis=0), NT).astype(BF)
        wg_ref[0, r] = t[:, : 2 * BLK]
        wg_ref[1, r] = t[:, 2 * BLK :]
        t = dot(g_ref[r], jnp.concatenate(pick(cols, 2, rows, r, hid), axis=0), NT)
        wg_ref[2, r] = t.astype(BF)

    looped(rows, 4, terms)


def last_kernel(cols, sec, a_ref, g_ref, gin_old, w_ref, fa, fb, hid, gin_ref, wg_ref, gh, gg, gu, gn):
    @pl.when(sec[0] == sec[1] - 1)
    def _():
        terms_into(cols, a_ref, g_ref, fa, fb, hid, wg_ref)

        def keep_old(r):
            gin_ref[r] = gin_old[r]

        looped(a_ref.shape[0], 4, keep_old)

    @pl.when(sec[0] < sec[1] - 1)
    def _():
        backward_into(cols, a_ref, g_ref, w_ref, fa, fb, gh, gg, gu, gn, gin_ref)
        terms_into(cols, a_ref, g_ref, gg, gu, hid, wg_ref)


VMEM = pl.BlockSpec(memory_space=pltpu.VMEM)
ANY = pl.BlockSpec(memory_space=pl.ANY)
LIMIT = 58 * 2**20


def call(kernel, cols, sec, arrays, outs, scratch):
    return pl.pallas_call(
        kernel,
        out_shape=[jax.ShapeDtypeStruct(s, d) for s, d in outs],
        in_specs=[pl.BlockSpec(memory_space=pltpu.SMEM)] * 2 + [VMEM] * len(arrays),
        out_specs=[VMEM] * len(outs),
        scratch_shapes=[pltpu.VMEM(s, d) for s, d in scratch],
        compiler_params=pltpu.CompilerParams(vmem_limit_bytes=LIMIT),
    )(cols, sec, *arrays)


def places(n):
    half = n // 2
    me = lax.axis_index("zero")
    low = lax.rem(me, 2)
    mine = lax.div(me, 2)
    return me, me + 1 - 2 * low, half, low, mine


def remote(src, dst, send, recv, where):
    return pltpu.make_async_remote_copy(
        src_ref=src, dst_ref=dst, send_sem=send, recv_sem=recv,
        device_id=where, device_id_type=pl.DeviceIdType.MESH,
    )


def greet(targets):
    barrier = pltpu.get_barrier_semaphore()
    for t in targets:
        pl.semaphore_signal(barrier, inc=1, device_id=t, device_id_type=pl.DeviceIdType.MESH)
    pl.semaphore_wait(barrier, len(targets))


def gather_kernel(n, sections, own, x_ref, c_ref, out, xt_ref, ct_ref, local, zs, zr, ys, yr, go):
    me, partner, half, low, mine = places(n)
    sec = lax.axis_index("section")
    other = {"section": sections - 1 - sec}
    r_own = own.shape[1]

    def peer(d):
        return lax.rem(mine + d, half) * 2 + low

    def slot(m, who):
        return out.at[m, pl.ds(who * r_own, r_own)]

    greet([{"zero": peer(d)} for d in range(1, half)] + [{"zero": partner}, other])
    stays = [pltpu.make_async_copy(own.at[m], slot(m, me), local.at[m]) for m in range(3)]
    for c in stays:
        c.start()

    def transposed(p, carry):
        lanes = pl.ds(pl.multiple_of(p * 2 * BLK, 2 * BLK), 2 * BLK)
        for src, dst in ((x_ref, xt_ref), (c_ref, ct_ref)):
            t = src[:, lanes].T
            dst[2 * p] = t[:BLK]
            dst[2 * p + 1] = t[BLK:]
        return carry

    @pl.when(sec == sections - 1)
    def _():
        pl.semaphore_wait(go, 1)

    sent = []
    for m in range(3):
        for d in range(1, half):
            c = remote(own.at[m], slot(m, me), zs.at[m, d], zr.at[m, d], {"zero": peer(d)})
            c.start()
            sent.append(c)
        c = remote(own.at[m], slot(m, me), ys.at[m, 0], yr.at[m, 0], {"zero": partner})
        c.start()
        sent.append(c)
    lax.fori_loop(0, x_ref.shape[1] // (2 * BLK), transposed, 0)
    for m in range(3):
        for d in range(1, half):
            who = lax.rem(mine + half - d, half) * 2 + low
            remote(own.at[m], slot(m, who), zs.at[m, d], zr.at[m, d], {"zero": partner}).wait_recv()
            c = remote(slot(m, who), slot(m, who), ys.at[m, d], yr.at[m, d], {"zero": partner})
            c.start()
            sent.append(c)
    for m in range(3):
        for d in range(half):
            who = lax.rem(mine + half - d, half) * 2 + 1 - low
            remote(own.at[m], slot(m, who), ys.at[m, d], yr.at[m, d], {"zero": partner}).wait_recv()

    @pl.when(sec == 0)
    def _():
        pl.semaphore_signal(go, inc=1, device_id=other, device_id_type=pl.DeviceIdType.MESH)

    for c in sent:
        c.wait_send()
    for c in stays:
        c.wait()


def reduce_kernel(n, terms, out_t, gin_t, sums, out_ref, gin_ref, near, mid, far, ys, yr, zs, zr):
    me, partner, half, low, mine = places(n)
    r_own = sums.shape[1]
    greet([{"zero": lax.rem(mine + d, half) * 2 + low} for d in range(1, half)] + [{"zero": partner}])
    order = list(range(1, half)) + [0]
    sent = []

    def position(d):
        return lax.rem(mine + d, half) * 2

    for d in order:
        for m in range(3):
            src = terms.at[m, pl.ds((position(d) + 1 - low) * r_own, r_own)]
            c = remote(src, near.at[d, m], ys.at[d, m], yr.at[d, m], {"zero": partner})
            c.start()
            sent.append(c)

    def transposed(p, carry):
        lanes = pl.ds(pl.multiple_of(p * 2 * BLK, 2 * BLK), 2 * BLK)
        for src, dst in ((out_t, out_ref), (gin_t, gin_ref)):
            dst[:, lanes] = jnp.concatenate([src[2 * p], src[2 * p + 1]], axis=0).T
        return carry

    pairs = out_t.shape[0] // 2
    todo = len(order)
    for i, d in enumerate(order):
        lax.fori_loop(i * pairs // todo, (i + 1) * pairs // todo, transposed, 0)
        for m in range(3):
            remote(near.at[d, m], near.at[d, m], ys.at[d, m], yr.at[d, m], {"zero": partner}).wait_recv()
            first = (position(d) + low) * r_own

            def add(r, carry):
                both = terms[m, first + r].astype(F32) + near[d, m, r].astype(F32)
                mid[d, m, r] = both.astype(BF)
                return carry

            lax.fori_loop(0, r_own, add, 0)
            if d:
                c = remote(
                    mid.at[d, m], far.at[d, m], zs.at[d, m], zr.at[d, m],
                    {"zero": position(d) + low},
                )
                c.start()
                sent.append(c)
    for m in range(3):
        for d in range(1, half):
            remote(mid.at[d, m], far.at[d, m], zs.at[d, m], zr.at[d, m], {"zero": partner}).wait_recv()

        def total(r, carry):
            value = mid[0, m, r].astype(F32)
            for d in range(1, half):
                value = value + far[d, m, r].astype(F32)
            sums[m, r] = value
            return carry

        lax.fori_loop(0, r_own, total, 0)
    for c in sent:
        c.wait_send()


def gather_all(own, x, c, n, sections):
    tokens, width = x.shape
    three, r_own, blk, two = own.shape
    half = n // 2
    tall = (width // BLK, BLK, tokens)
    sems = pltpu.SemaphoreType.DMA((3, half))
    return pl.pallas_call(
        lambda *refs: gather_kernel(n, sections, *refs),
        out_shape=[
            jax.ShapeDtypeStruct((three, n * r_own, blk, two), BF),
            jax.ShapeDtypeStruct(tall, BF),
            jax.ShapeDtypeStruct(tall, BF),
        ],
        in_specs=[ANY, VMEM, VMEM],
        out_specs=[ANY, VMEM, VMEM],
        scratch_shapes=[pltpu.SemaphoreType.DMA((3,)), sems, sems, sems, sems, pltpu.SemaphoreType.REGULAR],
        compiler_params=pltpu.CompilerParams(collective_id=0, has_side_effects=True, vmem_limit_bytes=LIMIT),
    )(own, x, c)


def reduce_all(terms, out_t, gin_t, n):
    three, rows, blk, two = terms.shape
    half = n // 2
    r_own = rows // n
    tokens = out_t.shape[2]
    flat = jax.ShapeDtypeStruct((tokens, rows * blk), BF)
    held = pltpu.VMEM((half, 3, r_own, blk, two), BF)
    sems = pltpu.SemaphoreType.DMA((half, 3))
    return pl.pallas_call(
        lambda *refs: reduce_kernel(n, *refs),
        out_shape=[jax.ShapeDtypeStruct((three, r_own, blk, two), F32), flat, flat],
        in_specs=[VMEM] * 3,
        out_specs=[VMEM] * 3,
        scratch_shapes=[held, held, held, sems, sems, sems, sems],
        compiler_params=pltpu.CompilerParams(collective_id=1, has_side_effects=True, vmem_limit_bytes=LIMIT),
    )(terms, out_t, gin_t)


def shards(inputs, cotangent, weights, keep, columns):
    sections = lax.axis_size("section")
    section_id = lax.axis_index("section")
    n = lax.axis_size("zero")
    tokens, width = inputs.shape
    rows = width // BLK
    norm_factor = 1.0 / math.sqrt(tokens * n)
    own_keep = keep[0]
    own_rows = own_keep.shape[1]
    masked = weights[0] * own_keep[..., None].astype(BF)
    own = masked.reshape(3, own_rows, 2, BLK, BLK).transpose(0, 1, 3, 2, 4)
    own = own.reshape(3, own_rows, BLK, 2 * BLK)
    mats, start, cot = gather_all(own, inputs, cotangent, n, sections)
    cols = columns[0].reshape(-1)
    sec = jnp.stack([section_id, jnp.int32(sections)]).astype(jnp.int32)
    tall = (rows, BLK, tokens)
    wide = (NBC, BLK, tokens)
    (out,) = call(
        first_kernel, cols, sec, (start, mats), [(tall, BF)],
        [(tall, BF), (wide, F32), (wide, F32), (wide, BF)],
    )
    moved = lax.ppermute(out, "section", [(0, 1)])
    current = jnp.where(section_id == 0, start, moved)
    out, gin, fa, fb, hid = call(
        middle_kernel, cols, sec, (current, cot, mats),
        [(tall, BF), (tall, BF), (wide, BF), (wide, BF), (wide, BF)],
        [(tall, BF), (wide, F32), (wide, F32), (wide, BF), (wide, BF), (tall, F32)],
    )
    moved = lax.ppermute(gin, "section", [(1, 0)])
    upstream = jnp.where(section_id == sections - 1, cot, moved)
    gin, terms = call(
        last_kernel, cols, sec, (current, upstream, gin, mats, fa, fb, hid),
        [(tall, BF), ((3, rows, BLK, 2 * BLK), BF)],
        [(wide, F32), (wide, BF), (wide, BF), (tall, F32)],
    )
    summed, out, gin = reduce_all(terms, out, gin, n)
    grad = summed.reshape(3, own_rows, BLK, 2, BLK).transpose(0, 1, 3, 2, 4)
    grad = grad.reshape(3, own_rows, 2, BLK * BLK)
    grad = grad * own_keep[..., None].astype(F32) * norm_factor
    return (out[None], gin[None], grad[None])


def solution(mesh):
    return jax.shard_map(
        shards,
        mesh=mesh,
        in_specs=(
            P(("groups", "zero"), None),
            P(("groups", "zero"), None),
            P("section", None, "zero", None, None),
            P("section", None, "zero", None),
            P("section", None, None, None),
        ),
        out_specs=(
            P("section", ("groups", "zero"), None),
            P("section", ("groups", "zero"), None),
            P("section", None, ("groups", "zero"), None, None),
        ),
        check_vma=False,
    )
```

```python
import math

import jax
import jax.numpy as jnp
from jax import lax
from jax.experimental import pallas as pl
from jax.experimental.pallas import tpu as pltpu
from jax.sharding import PartitionSpec as P

FF = 11008
BLK = 64
NBC = FF // BLK
BF = jnp.bfloat16
F32 = jnp.float32
epsilon = 1e-05

TN = (((0,), (0,)), ((), ()))
NT = (((1,), (1,)), ((), ()))


def dot(a, b, dims=(((1,), (0,)), ((), ()))):
    return lax.dot_general(a, b, dims, preferred_element_type=F32)


def total_rows(acc):
    return jnp.sum(acc, axis=0, keepdims=True)


def fold(value):
    return jnp.sum(value.reshape(-1, 8, value.shape[-1]), axis=0)


def looped(count, unroll, body):
    def step(i, carry):
        for k in range(unroll):
            body(i * unroll + k)
        return carry

    lax.fori_loop(0, count // unroll, step, 0)


def norm_scale(a_ref):
    rows, blk, tokens = a_ref.shape

    def add(i, acc):
        for k in range(4):
            v = a_ref[i * 4 + k].astype(F32)
            acc = acc + fold(v * v)
        return acc

    acc = lax.fori_loop(0, rows // 4, add, jnp.zeros((8, tokens), F32))
    return lax.rsqrt(total_rows(acc) / (rows * blk) + epsilon)


def column(cols, m, r, k, rows):
    return cols[(m * rows + r) * 2 + k]


def clear(*refs):
    def body(c):
        for ref in refs:
            ref[c] = jnp.zeros(ref.shape[1:], ref.dtype)

    looped(NBC, 4, body)


def spread(cols, m, rows, r, w, x, out):
    res = dot(w, x, TN)
    for k in range(2):
        c = column(cols, m, r, k, rows)
        out[c] += res[k * BLK : (k + 1) * BLK]


def pick(cols, m, rows, r, src):
    return [src[column(cols, m, r, k, rows)] for k in range(2)]


def forward_into(cols, a_ref, w_ref, out_ref, xn, pg, pu, hid, fa=None, fb=None):
    rows = a_ref.shape[0]
    recip = norm_scale(a_ref)

    def normed(r):
        xn[r] = (a_ref[r].astype(F32) * recip).astype(BF)

    looped(rows, 4, normed)
    clear(pg, pu)

    def up(r):
        x = xn[r]
        spread(cols, 0, rows, r, w_ref[0, r], x, pg)
        spread(cols, 1, rows, r, w_ref[1, r], x, pu)

    looped(rows, 4, up)

    def act(c):
        g = pg[c]
        u = pu[c]
        s = 1.0 / (1.0 + jnp.exp(-g))
        silu = g * s
        hid[c] = (silu * u).astype(BF)
        if fa is not None:
            fa[c] = (u * s * (1.0 + g * (1.0 - s))).astype(BF)
            fb[c] = silu.astype(BF)

    looped(NBC, 2, act)

    def down(r):
        o = dot(w_ref[2, r], jnp.concatenate(pick(cols, 2, rows, r, hid), axis=0))
        out_ref[r] = (a_ref[r].astype(F32) + o).astype(BF)

    looped(rows, 4, down)


def spread_back(cols, g_ref, w_ref, fa, fb, gh, gg, gu):
    rows = g_ref.shape[0]
    clear(gh)
    looped(rows, 4, lambda r: spread(cols, 2, rows, r, w_ref[2, r], g_ref[r], gh))

    def act(c):
        v = gh[c]
        gg[c] = (v * fa[c].astype(F32)).astype(BF)
        gu[c] = (v * fb[c].astype(F32)).astype(BF)

    looped(NBC, 2, act)


def back_sums(cols, a_ref, recip, w_ref, gg, gu, gn, first, last, acc):
    rows = a_ref.shape[0]

    def back(i, acc):
        for k in range(4):
            r = i * 4 + k
            right = pick(cols, 0, rows, r, gg) + pick(cols, 1, rows, r, gu)
            left = jnp.concatenate([w_ref[0, r], w_ref[1, r]], axis=1)
            v = dot(left, jnp.concatenate(right, axis=0))
            gn[r] = v
            acc = acc + fold(v * (a_ref[r].astype(F32) * recip))
        return acc

    return lax.fori_loop(first // 4, last // 4, back, acc)


def grad_rows(a_ref, g_ref, recip, gn, inner, r):
    q = a_ref[r].astype(F32) * recip
    return (g_ref[r].astype(F32) + recip * (gn[r] - q * inner)).astype(BF)


def backward_into(cols, a_ref, g_ref, w_ref, fa, fb, gh, gg, gu, gn, gin_ref):
    rows, blk, tokens = a_ref.shape
    recip = norm_scale(a_ref)
    spread_back(cols, g_ref, w_ref, fa, fb, gh, gg, gu)
    acc = back_sums(cols, a_ref, recip, w_ref, gg, gu, gn, 0, rows, jnp.zeros((8, tokens), F32))
    inner = total_rows(acc) / (rows * blk)

    def finish(r):
        gin_ref[r] = grad_rows(a_ref, g_ref, recip, gn, inner, r)

    looped(rows, 4, finish)


def first_kernel(cols, sec, a_ref, w_ref, out_ref, xn, pg, pu, hid):
    @pl.when(sec[0] < sec[1] - 1)
    def _():
        forward_into(cols, a_ref, w_ref, out_ref, xn, pg, pu, hid)


def middle_kernel(cols, sec, a_ref, g_ref, w_ref, out_ref, gin_ref, fa, fb, hid, xn, pg, pu, ga, gb, gn):
    forward_into(cols, a_ref, w_ref, out_ref, xn, pg, pu, hid, fa, fb)

    @pl.when(sec[0] == sec[1] - 1)
    def _():
        backward_into(cols, a_ref, g_ref, w_ref, fa, fb, pg, ga, gb, gn, gin_ref)

        def keep_grads(c):
            fa[c] = ga[c]
            fb[c] = gb[c]

        looped(NBC, 4, keep_grads)


def terms_at(cols, a_ref, g_ref, recip, gg, gu, hid, wg_ref, r):
    rows = a_ref.shape[0]
    x = (a_ref[r].astype(F32) * recip).astype(BF)
    right = pick(cols, 0, rows, r, gg) + pick(cols, 1, rows, r, gu)
    t = dot(x, jnp.concatenate(right, axis=0), NT).astype(BF)
    wg_ref[0, r] = t[:, : 2 * BLK]
    wg_ref[1, r] = t[:, 2 * BLK :]
    t = dot(g_ref[r], jnp.concatenate(pick(cols, 2, rows, r, hid), axis=0), NT)
    wg_ref[2, r] = t.astype(BF)


def last_kernel(cols, sec, g_ref, w_ref, fa, fb, gg, gu, gh):
    @pl.when(sec[0] == sec[1] - 1)
    def _():
        def keep(c):
            gg[c] = fa[c]
            gu[c] = fb[c]

        looped(NBC, 4, keep)

    @pl.when(sec[0] < sec[1] - 1)
    def _():
        spread_back(cols, g_ref, w_ref, fa, fb, gh, gg, gu)


VMEM = pl.BlockSpec(memory_space=pltpu.VMEM)
ANY = pl.BlockSpec(memory_space=pl.ANY)
LIMIT = 58 * 2**20


def call(kernel, cols, sec, arrays, outs, scratch):
    return pl.pallas_call(
        kernel,
        out_shape=[jax.ShapeDtypeStruct(s, d) for s, d in outs],
        in_specs=[pl.BlockSpec(memory_space=pltpu.SMEM)] * 2 + [VMEM] * len(arrays),
        out_specs=[VMEM] * len(outs),
        scratch_shapes=[pltpu.VMEM(s, d) for s, d in scratch],
        compiler_params=pltpu.CompilerParams(vmem_limit_bytes=LIMIT),
    )(cols, sec, *arrays)


def places(n):
    half = n // 2
    me = lax.axis_index("zero")
    low = lax.rem(me, 2)
    mine = lax.div(me, 2)
    return me, me + 1 - 2 * low, half, low, mine


def remote(src, dst, send, recv, where):
    return pltpu.make_async_remote_copy(
        src_ref=src, dst_ref=dst, send_sem=send, recv_sem=recv,
        device_id=where, device_id_type=pl.DeviceIdType.MESH,
    )


def greet(targets):
    barrier = pltpu.get_barrier_semaphore()
    for t in targets:
        pl.semaphore_signal(barrier, inc=1, device_id=t, device_id_type=pl.DeviceIdType.MESH)
    pl.semaphore_wait(barrier, len(targets))


def gather_kernel(n, sections, own, x_ref, c_ref, out, xt_ref, ct_ref, local, zs, zr, ys, yr, go):
    me, partner, half, low, mine = places(n)
    sec = lax.axis_index("section")
    other = {"section": sections - 1 - sec}
    r_own = own.shape[1]

    def peer(d):
        return lax.rem(mine + d, half) * 2 + low

    def slot(m, who):
        return out.at[m, pl.ds(who * r_own, r_own)]

    greet([{"zero": peer(d)} for d in range(1, half)] + [{"zero": partner}, other])
    stays = [pltpu.make_async_copy(own.at[m], slot(m, me), local.at[m]) for m in range(3)]
    for c in stays:
        c.start()

    def transposed(p, carry):
        lanes = pl.ds(pl.multiple_of(p * 2 * BLK, 2 * BLK), 2 * BLK)
        for src, dst in ((x_ref, xt_ref), (c_ref, ct_ref)):
            t = src[:, lanes].T
            dst[2 * p] = t[:BLK]
            dst[2 * p + 1] = t[BLK:]
        return carry

    @pl.when(sec == sections - 1)
    def _():
        pl.semaphore_wait(go, 1)

    sent = []
    for m in range(3):
        for d in range(1, half):
            c = remote(own.at[m], slot(m, me), zs.at[m, d], zr.at[m, d], {"zero": peer(d)})
            c.start()
            sent.append(c)
        c = remote(own.at[m], slot(m, me), ys.at[m, 0], yr.at[m, 0], {"zero": partner})
        c.start()
        sent.append(c)
    pairs = x_ref.shape[1] // (2 * BLK)
    steps = 3 * (half - 1)
    for m in range(3):
        for d in range(1, half):
            at = m * (half - 1) + d - 1
            lax.fori_loop(at * pairs // steps, (at + 1) * pairs // steps, transposed, 0)
            who = lax.rem(mine + half - d, half) * 2 + low
            remote(own.at[m], slot(m, who), zs.at[m, d], zr.at[m, d], {"zero": partner}).wait_recv()
            c = remote(slot(m, who), slot(m, who), ys.at[m, d], yr.at[m, d], {"zero": partner})
            c.start()
            sent.append(c)

    @pl.when(sec == 0)
    def _():
        pl.semaphore_signal(go, inc=1, device_id=other, device_id_type=pl.DeviceIdType.MESH)

    for m in range(3):
        for d in range(half):
            who = lax.rem(mine + half - d, half) * 2 + 1 - low
            remote(own.at[m], slot(m, who), ys.at[m, d], yr.at[m, d], {"zero": partner}).wait_recv()

    for c in sent:
        c.wait_send()
    for c in stays:
        c.wait()


def reduce_kernel(
    n, sections, cols, a_ref, g_ref, w_ref, gg, gu, hid, gin_old, out_t, sums, out_ref, gin_ref,
    terms, gn, part, near, mid, far, ys, yr, zs, zr
):
    me, partner, half, low, mine = places(n)
    sec = lax.axis_index("section")
    rows, blk, tokens = a_ref.shape
    r_own = sums.shape[1]
    greet([{"zero": lax.rem(mine + d, half) * 2 + low} for d in range(1, half)] + [{"zero": partner}])
    order = list(range(1, half)) + [0]
    todo = len(order)
    sent = []
    recip = norm_scale(a_ref)
    part[...] = jnp.zeros_like(part)

    def position(d):
        return lax.rem(mine + d, half) * 2

    def block_of(who):
        def body(r):
            terms_at(cols, a_ref, g_ref, recip, gg, gu, hid, terms, who * r_own + r)

        looped(r_own, 4, body)

    for d in order:
        who = position(d) + 1 - low
        block_of(who)
        for m in range(3):
            src = terms.at[m, pl.ds(who * r_own, r_own)]
            c = remote(src, near.at[d, m], ys.at[d, m], yr.at[d, m], {"zero": partner})
            c.start()
            sent.append(c)

    for i, d in enumerate(order):
        block_of(position(d) + low)

        @pl.when(sec < sections - 1)
        def _():
            first, last = (i * rows // todo, (i + 1) * rows // todo)
            part[...] = back_sums(cols, a_ref, recip, w_ref, gg, gu, gn, first, last, part[...])

        for m in range(3):
            remote(near.at[d, m], near.at[d, m], ys.at[d, m], yr.at[d, m], {"zero": partner}).wait_recv()
            first = (position(d) + low) * r_own

            def add(r, carry):
                both = terms[m, first + r].astype(F32) + near[d, m, r].astype(F32)
                mid[d, m, r] = both.astype(BF)
                return carry

            lax.fori_loop(0, r_own, add, 0)
            if d:
                c = remote(
                    mid.at[d, m], far.at[d, m], zs.at[d, m], zr.at[d, m],
                    {"zero": position(d) + low},
                )
                c.start()
                sent.append(c)

    def flipped(dst, rows_of):
        def body(p, carry):
            lanes = pl.ds(pl.multiple_of(p * 2 * BLK, 2 * BLK), 2 * BLK)
            dst[:, lanes] = jnp.concatenate([rows_of(2 * p), rows_of(2 * p + 1)], axis=0).T
            return carry

        lax.fori_loop(0, rows // 2, body, 0)

    flipped(out_ref, lambda r: out_t[r])

    @pl.when(sec == sections - 1)
    def _():
        flipped(gin_ref, lambda r: gin_old[r])

    @pl.when(sec < sections - 1)
    def _():
        inner = total_rows(part[...]) / (rows * blk)
        flipped(gin_ref, lambda r: grad_rows(a_ref, g_ref, recip, gn, inner, r))

    for m in range(3):
        for d in range(1, half):
            remote(mid.at[d, m], far.at[d, m], zs.at[d, m], zr.at[d, m], {"zero": partner}).wait_recv()

        def total(r, carry):
            value = mid[0, m, r].astype(F32)
            for d in range(1, half):
                value = value + far[d, m, r].astype(F32)
            sums[m, r] = value
            return carry

        lax.fori_loop(0, r_own, total, 0)
    for c in sent:
        c.wait_send()


def gather_all(own, x, c, n, sections):
    tokens, width = x.shape
    three, r_own, blk, two = own.shape
    half = n // 2
    tall = (width // BLK, BLK, tokens)
    sems = pltpu.SemaphoreType.DMA((3, half))
    return pl.pallas_call(
        lambda *refs: gather_kernel(n, sections, *refs),
        out_shape=[
            jax.ShapeDtypeStruct((three, n * r_own, blk, two), BF),
            jax.ShapeDtypeStruct(tall, BF),
            jax.ShapeDtypeStruct(tall, BF),
        ],
        in_specs=[ANY, VMEM, VMEM],
        out_specs=[ANY, VMEM, VMEM],
        scratch_shapes=[pltpu.SemaphoreType.DMA((3,)), sems, sems, sems, sems, pltpu.SemaphoreType.REGULAR],
        compiler_params=pltpu.CompilerParams(collective_id=0, has_side_effects=True, vmem_limit_bytes=LIMIT),
    )(own, x, c)


def reduce_all(n, sections, own_rows, cols, a, g, mats, gg, gu, hid, gin_old, out_t):
    three, rows, blk, two = mats.shape
    half = n // 2
    tokens = out_t.shape[2]
    flat = jax.ShapeDtypeStruct((tokens, rows * blk), BF)
    held = pltpu.VMEM((half, 3, own_rows, blk, two), BF)
    sems = pltpu.SemaphoreType.DMA((half, 3))
    return pl.pallas_call(
        lambda *refs: reduce_kernel(n, sections, *refs),
        out_shape=[jax.ShapeDtypeStruct((three, own_rows, blk, two), F32), flat, flat],
        in_specs=[pl.BlockSpec(memory_space=pltpu.SMEM)] + [VMEM] * 8,
        out_specs=[VMEM] * 3,
        scratch_shapes=[
            pltpu.VMEM(mats.shape, BF),
            pltpu.VMEM((rows, blk, tokens), F32),
            pltpu.VMEM((8, tokens), F32),
            held, held, held, sems, sems, sems, sems,
        ],
        compiler_params=pltpu.CompilerParams(collective_id=1, has_side_effects=True, vmem_limit_bytes=LIMIT),
    )(cols, a, g, mats, gg, gu, hid, gin_old, out_t)


def shards(inputs, cotangent, weights, keep, columns):
    sections = lax.axis_size("section")
    section_id = lax.axis_index("section")
    n = lax.axis_size("zero")
    tokens, width = inputs.shape
    rows = width // BLK
    norm_factor = 1.0 / math.sqrt(tokens * n)
    own_keep = keep[0]
    own_rows = own_keep.shape[1]
    masked = weights[0] * own_keep[..., None].astype(BF)
    own = masked.reshape(3, own_rows, 2, BLK, BLK).transpose(0, 1, 3, 2, 4)
    own = own.reshape(3, own_rows, BLK, 2 * BLK)
    mats, start, cot = gather_all(own, inputs, cotangent, n, sections)
    cols = columns[0].reshape(-1)
    sec = jnp.stack([section_id, jnp.int32(sections)]).astype(jnp.int32)
    tall = (rows, BLK, tokens)
    wide = (NBC, BLK, tokens)
    (out,) = call(
        first_kernel, cols, sec, (start, mats), [(tall, BF)],
        [(tall, BF), (wide, F32), (wide, F32), (wide, BF)],
    )
    moved = lax.ppermute(out, "section", [(0, 1)])
    current = jnp.where(section_id == 0, start, moved)
    out, gin, fa, fb, hid = call(
        middle_kernel, cols, sec, (current, cot, mats),
        [(tall, BF), (tall, BF), (wide, BF), (wide, BF), (wide, BF)],
        [(tall, BF), (wide, F32), (wide, F32), (wide, BF), (wide, BF), (tall, F32)],
    )
    moved = lax.ppermute(gin, "section", [(1, 0)])
    upstream = jnp.where(section_id == sections - 1, cot, moved)
    gg, gu = call(
        last_kernel, cols, sec, (upstream, mats, fa, fb), [(wide, BF), (wide, BF)], [(wide, F32)]
    )
    summed, out, gin = reduce_all(
        n, sections, own_rows, cols, current, upstream, mats, gg, gu, hid, gin, out
    )
    grad = summed.reshape(3, own_rows, BLK, 2, BLK).transpose(0, 1, 3, 2, 4)
    grad = grad.reshape(3, own_rows, 2, BLK * BLK)
    grad = grad * own_keep[..., None].astype(F32) * norm_factor
    return (out[None], gin[None], grad[None])


def solution(mesh):
    return jax.shard_map(
        shards,
        mesh=mesh,
        in_specs=(
            P(("groups", "zero"), None),
            P(("groups", "zero"), None),
            P("section", None, "zero", None, None),
            P("section", None, "zero", None),
            P("section", None, None, None),
        ),
        out_specs=(
            P("section", ("groups", "zero"), None),
            P("section", ("groups", "zero"), None),
            P("section", None, ("groups", "zero"), None, None),
        ),
        check_vma=False,
    )
```

```python
import math

import jax
import jax.numpy as jnp
from jax import lax
from jax.experimental import pallas as pl
from jax.experimental.pallas import tpu as pltpu
from jax.sharding import PartitionSpec as P

FF = 11008
BLK = 64
NBC = FF // BLK
BF = jnp.bfloat16
F32 = jnp.float32
epsilon = 1e-05

TN = (((0,), (0,)), ((), ()))
NT = (((1,), (1,)), ((), ()))


def dot(a, b, dims=(((1,), (0,)), ((), ()))):
    return lax.dot_general(a, b, dims, preferred_element_type=F32)


def total_rows(acc):
    return jnp.sum(acc, axis=0, keepdims=True)


def fold(value):
    return jnp.sum(value.reshape(-1, 8, value.shape[-1]), axis=0)


def looped(count, unroll, body):
    def step(i, carry):
        for k in range(unroll):
            body(i * unroll + k)
        return carry

    lax.fori_loop(0, count // unroll, step, 0)


def norm_scale(a_ref):
    rows, blk, tokens = a_ref.shape

    def add(i, acc):
        for k in range(4):
            v = a_ref[i * 4 + k].astype(F32)
            acc = acc + fold(v * v)
        return acc

    acc = lax.fori_loop(0, rows // 4, add, jnp.zeros((8, tokens), F32))
    return lax.rsqrt(total_rows(acc) / (rows * blk) + epsilon)


def column(cols, m, r, k, rows):
    return cols[(m * rows + r) * 2 + k]


def clear(*refs):
    def body(c):
        for ref in refs:
            ref[c] = jnp.zeros(ref.shape[1:], ref.dtype)

    looped(NBC, 4, body)


def spread(cols, m, rows, r, w, x, out):
    res = dot(w, x, TN)
    for k in range(2):
        c = column(cols, m, r, k, rows)
        out[c] += res[k * BLK : (k + 1) * BLK]


def pick(cols, m, rows, r, src):
    return [src[column(cols, m, r, k, rows)] for k in range(2)]


def forward_into(cols, a_ref, w_ref, out_ref, xn, pg, pu, hid, fa=None, fb=None):
    rows = a_ref.shape[0]
    recip = norm_scale(a_ref)

    def normed(r):
        xn[r] = (a_ref[r].astype(F32) * recip).astype(BF)

    looped(rows, 4, normed)
    clear(pg, pu)

    def up(r):
        x = xn[r]
        spread(cols, 0, rows, r, w_ref[0, r], x, pg)
        spread(cols, 1, rows, r, w_ref[1, r], x, pu)

    looped(rows, 4, up)

    def act(c):
        g = pg[c]
        u = pu[c]
        s = 1.0 / (1.0 + jnp.exp(-g))
        silu = g * s
        hid[c] = (silu * u).astype(BF)
        if fa is not None:
            fa[c] = (u * s * (1.0 + g * (1.0 - s))).astype(BF)
            fb[c] = silu.astype(BF)

    looped(NBC, 2, act)

    def down(r):
        o = dot(w_ref[2, r], jnp.concatenate(pick(cols, 2, rows, r, hid), axis=0))
        out_ref[r] = (a_ref[r].astype(F32) + o).astype(BF)

    looped(rows, 4, down)


def spread_back(cols, g_ref, w_ref, fa, fb, gh, gg, gu):
    rows = g_ref.shape[0]
    clear(gh)
    looped(rows, 4, lambda r: spread(cols, 2, rows, r, w_ref[2, r], g_ref[r], gh))

    def act(c):
        v = gh[c]
        gg[c] = (v * fa[c].astype(F32)).astype(BF)
        gu[c] = (v * fb[c].astype(F32)).astype(BF)

    looped(NBC, 2, act)


def back_sums(cols, a_ref, recip, w_ref, gg, gu, gn, first, last, acc):
    rows = a_ref.shape[0]

    def back(i, acc):
        for k in range(4):
            r = i * 4 + k
            right = pick(cols, 0, rows, r, gg) + pick(cols, 1, rows, r, gu)
            left = jnp.concatenate([w_ref[0, r], w_ref[1, r]], axis=1)
            v = dot(left, jnp.concatenate(right, axis=0))
            gn[r] = v
            acc = acc + fold(v * (a_ref[r].astype(F32) * recip))
        return acc

    return lax.fori_loop(first // 4, last // 4, back, acc)


def grad_rows(a_ref, g_ref, recip, gn, inner, r):
    q = a_ref[r].astype(F32) * recip
    return (g_ref[r].astype(F32) + recip * (gn[r] - q * inner)).astype(BF)


def first_kernel(cols, sec, a_ref, w_ref, out_ref, xn, pg, pu, hid):
    @pl.when(sec[0] < sec[1] - 1)
    def _():
        forward_into(cols, a_ref, w_ref, out_ref, xn, pg, pu, hid)


def middle_kernel(cols, sec, a_ref, g_ref, w_ref, out_ref, fa, fb, hid, xn, pg, pu):
    forward_into(cols, a_ref, w_ref, out_ref, xn, pg, pu, hid, fa, fb)

    @pl.when(sec[0] == sec[1] - 1)
    def _():
        spread_back(cols, g_ref, w_ref, fa, fb, pg, fa, fb)


def terms_at(cols, a_ref, g_ref, recip, gg, gu, hid, wg_ref, r):
    rows = a_ref.shape[0]
    x = (a_ref[r].astype(F32) * recip).astype(BF)
    right = pick(cols, 0, rows, r, gg) + pick(cols, 1, rows, r, gu)
    t = dot(x, jnp.concatenate(right, axis=0), NT).astype(BF)
    wg_ref[0, r] = t[:, : 2 * BLK]
    wg_ref[1, r] = t[:, 2 * BLK :]
    t = dot(g_ref[r], jnp.concatenate(pick(cols, 2, rows, r, hid), axis=0), NT)
    wg_ref[2, r] = t.astype(BF)


def last_kernel(cols, sec, g_ref, w_ref, fa, fb, gg, gu, gh):
    @pl.when(sec[0] < sec[1] - 1)
    def _():
        spread_back(cols, g_ref, w_ref, fa, fb, gh, gg, gu)


VMEM = pl.BlockSpec(memory_space=pltpu.VMEM)
ANY = pl.BlockSpec(memory_space=pl.ANY)
LIMIT = 58 * 2**20


def call(kernel, cols, sec, arrays, outs, scratch):
    return pl.pallas_call(
        kernel,
        out_shape=[jax.ShapeDtypeStruct(s, d) for s, d in outs],
        in_specs=[pl.BlockSpec(memory_space=pltpu.SMEM)] * 2 + [VMEM] * len(arrays),
        out_specs=[VMEM] * len(outs),
        scratch_shapes=[pltpu.VMEM(s, d) for s, d in scratch],
        compiler_params=pltpu.CompilerParams(vmem_limit_bytes=LIMIT),
    )(cols, sec, *arrays)


def places(n):
    half = n // 2
    me = lax.axis_index("zero")
    low = lax.rem(me, 2)
    mine = lax.div(me, 2)
    return me, me + 1 - 2 * low, half, low, mine


def remote(src, dst, send, recv, where):
    return pltpu.make_async_remote_copy(
        src_ref=src, dst_ref=dst, send_sem=send, recv_sem=recv,
        device_id=where, device_id_type=pl.DeviceIdType.MESH,
    )


def greet(targets):
    barrier = pltpu.get_barrier_semaphore()
    for t in targets:
        pl.semaphore_signal(barrier, inc=1, device_id=t, device_id_type=pl.DeviceIdType.MESH)
    pl.semaphore_wait(barrier, len(targets))


def gather_kernel(n, sections, own, x_ref, c_ref, out, xt_ref, ct_ref, local, zs, zr, ys, yr, go):
    me, partner, half, low, mine = places(n)
    sec = lax.axis_index("section")
    other = {"section": sections - 1 - sec}
    r_own = own.shape[1]

    def peer(d):
        return lax.rem(mine + d, half) * 2 + low

    def slot(m, who):
        return out.at[m, pl.ds(who * r_own, r_own)]

    greet([{"zero": peer(d)} for d in range(1, half)] + [{"zero": partner}, other])
    stays = [pltpu.make_async_copy(own.at[m], slot(m, me), local.at[m]) for m in range(3)]
    for c in stays:
        c.start()

    def transposed(p, carry):
        lanes = pl.ds(pl.multiple_of(p * 2 * BLK, 2 * BLK), 2 * BLK)
        for src, dst in ((x_ref, xt_ref), (c_ref, ct_ref)):
            t = src[:, lanes].T
            dst[2 * p] = t[:BLK]
            dst[2 * p + 1] = t[BLK:]
        return carry

    @pl.when(sec == sections - 1)
    def _():
        pl.semaphore_wait(go, 1)

    sent = []
    for m in range(3):
        for d in range(1, half):
            c = remote(own.at[m], slot(m, me), zs.at[m, d], zr.at[m, d], {"zero": peer(d)})
            c.start()
            sent.append(c)
        c = remote(own.at[m], slot(m, me), ys.at[m, 0], yr.at[m, 0], {"zero": partner})
        c.start()
        sent.append(c)
    pairs = x_ref.shape[1] // (2 * BLK)
    steps = 3 * (half - 1)
    for m in range(3):
        for d in range(1, half):
            at = m * (half - 1) + d - 1
            lax.fori_loop(at * pairs // steps, (at + 1) * pairs // steps, transposed, 0)
            who = lax.rem(mine + half - d, half) * 2 + low
            remote(own.at[m], slot(m, who), zs.at[m, d], zr.at[m, d], {"zero": partner}).wait_recv()
            c = remote(slot(m, who), slot(m, who), ys.at[m, d], yr.at[m, d], {"zero": partner})
            c.start()
            sent.append(c)

    @pl.when(sec == 0)
    def _():
        pl.semaphore_signal(go, inc=1, device_id=other, device_id_type=pl.DeviceIdType.MESH)

    for m in range(3):
        for d in range(half):
            who = lax.rem(mine + half - d, half) * 2 + 1 - low
            remote(own.at[m], slot(m, who), ys.at[m, d], yr.at[m, d], {"zero": partner}).wait_recv()

    for c in sent:
        c.wait_send()
    for c in stays:
        c.wait()


def flip(dst, rows_of, pairs):
    def body(p, carry):
        lanes = pl.ds(pl.multiple_of(p * 2 * BLK, 2 * BLK), 2 * BLK)
        dst[:, lanes] = jnp.concatenate([rows_of(2 * p), rows_of(2 * p + 1)], axis=0).T
        return carry

    lax.fori_loop(0, pairs, body, 0)


def hand_copy(gin_pass, sems, other):
    return remote(gin_pass, gin_pass, sems.at[0], sems.at[1], other)


def upper_kernel(n, sections, cols, a_ref, g_ref, w_ref, gg, gu, hid, out_t, sums, gin_ref, out_ref, gin_pass, *scratch):
    sec = lax.axis_index("section")
    other = {"section": sections - 1 - sec}
    hand = scratch[-1]
    pairs = a_ref.shape[0] // 2

    @pl.when(sec == sections - 1)
    def _():
        reduce_body(
            n, cols, a_ref, g_ref, w_ref, gg, gu, hid, sums, gin_ref, *scratch[:-1],
            upper=(out_t, out_ref, gin_pass, hand, other),
        )

    @pl.when(sec < sections - 1)
    def _():
        greet([other])
        flip(out_ref, lambda r: out_t[r], pairs)
        hand_copy(gin_pass, hand, other).wait_recv()


def lower_kernel(n, sections, cols, a_ref, g_ref, w_ref, gg, gu, hid, sums, gin_ref, *scratch):
    @pl.when(lax.axis_index("section") < sections - 1)
    def _():
        reduce_body(n, cols, a_ref, g_ref, w_ref, gg, gu, hid, sums, gin_ref, *scratch)


def reduce_body(
    n, cols, a_ref, g_ref, w_ref, gg, gu, hid, sums, gin_ref,
    terms, gn, near, mid, far, ys, yr, zs, zr, upper=None
):
    me, partner, half, low, mine = places(n)
    rows, blk, tokens = a_ref.shape
    r_own = sums.shape[1]
    peers = [{"zero": lax.rem(mine + d, half) * 2 + low} for d in range(1, half)]
    greet(peers + [{"zero": partner}] + ([upper[-1]] if upper else []))
    order = list(range(1, half)) + [0]
    todo = len(order)
    sent = []
    recip = norm_scale(a_ref)
    part = jnp.zeros((8, tokens), F32)

    def position(d):
        return lax.rem(mine + d, half) * 2

    def block_of(who):
        def body(r):
            terms_at(cols, a_ref, g_ref, recip, gg, gu, hid, terms, who * r_own + r)

        looped(r_own, 4, body)

    for i, d in enumerate(order):
        if i == 2 and upper:
            part = back_sums(cols, a_ref, recip, w_ref, gg, gu, gn, 0, rows, part)
            inner = total_rows(part) / (rows * blk)
            out_t, out_ref, gin_pass, hand, other = upper

            def finish(r):
                gin_pass[r] = grad_rows(a_ref, g_ref, recip, gn, inner, r)

            looped(rows, 4, finish)
            c = hand_copy(gin_pass, hand, other)
            c.start()
            sent.append(c)
        who = position(d) + 1 - low
        block_of(who)
        for m in range(3):
            src = terms.at[m, pl.ds(who * r_own, r_own)]
            c = remote(src, near.at[d, m], ys.at[d, m], yr.at[d, m], {"zero": partner})
            c.start()
            sent.append(c)

    for i, d in enumerate(order):
        block_of(position(d) + low)
        if not upper:
            first, last = (i * rows // todo, (i + 1) * rows // todo)
            part = back_sums(cols, a_ref, recip, w_ref, gg, gu, gn, first, last, part)
        for m in range(3):
            remote(near.at[d, m], near.at[d, m], ys.at[d, m], yr.at[d, m], {"zero": partner}).wait_recv()
            first = (position(d) + low) * r_own

            def add(r, carry):
                both = terms[m, first + r].astype(F32) + near[d, m, r].astype(F32)
                mid[d, m, r] = both.astype(BF)
                return carry

            lax.fori_loop(0, r_own, add, 0)
            if d:
                c = remote(
                    mid.at[d, m], far.at[d, m], zs.at[d, m], zr.at[d, m],
                    {"zero": position(d) + low},
                )
                c.start()
                sent.append(c)

    if upper:
        out_t, out_ref, gin_pass, hand, other = upper
        flip(out_ref, lambda r: out_t[r], rows // 2)
        flip(gin_ref, lambda r: gin_pass[r], rows // 2)
    else:
        inner = total_rows(part) / (rows * blk)
        flip(gin_ref, lambda r: grad_rows(a_ref, g_ref, recip, gn, inner, r), rows // 2)

    for m in range(3):
        for d in range(1, half):
            remote(mid.at[d, m], far.at[d, m], zs.at[d, m], zr.at[d, m], {"zero": partner}).wait_recv()

        def total(r, carry):
            value = mid[0, m, r].astype(F32)
            for d in range(1, half):
                value = value + far[d, m, r].astype(F32)
            sums[m, r] = value
            return carry

        lax.fori_loop(0, r_own, total, 0)
    for c in sent:
        c.wait_send()


def gather_all(own, x, c, n, sections):
    tokens, width = x.shape
    three, r_own, blk, two = own.shape
    half = n // 2
    tall = (width // BLK, BLK, tokens)
    sems = pltpu.SemaphoreType.DMA((3, half))
    return pl.pallas_call(
        lambda *refs: gather_kernel(n, sections, *refs),
        out_shape=[
            jax.ShapeDtypeStruct((three, n * r_own, blk, two), BF),
            jax.ShapeDtypeStruct(tall, BF),
            jax.ShapeDtypeStruct(tall, BF),
        ],
        in_specs=[ANY, VMEM, VMEM],
        out_specs=[ANY, VMEM, VMEM],
        scratch_shapes=[pltpu.SemaphoreType.DMA((3,)), sems, sems, sems, sems, pltpu.SemaphoreType.REGULAR],
        compiler_params=pltpu.CompilerParams(collective_id=0, has_side_effects=True, vmem_limit_bytes=LIMIT),
    )(own, x, c)


def reduce_all(kernel, ident, n, sections, own_rows, cols, a, g, mats, gg, gu, hid, out_t=None):
    three, rows, blk, two = mats.shape
    half = n // 2
    tokens = a.shape[2]
    flat = jax.ShapeDtypeStruct((tokens, rows * blk), BF)
    held = pltpu.VMEM((half, 3, own_rows, blk, two), BF)
    sems = pltpu.SemaphoreType.DMA((half, 3))
    outs = [jax.ShapeDtypeStruct((three, own_rows, blk, two), F32), flat]
    arrays = [a, g, mats, gg, gu, hid]
    scratch = [pltpu.VMEM(mats.shape, BF), pltpu.VMEM((rows, blk, tokens), F32)]
    scratch += [held, held, held, sems, sems, sems, sems]
    if out_t is not None:
        outs += [flat, jax.ShapeDtypeStruct(a.shape, BF)]
        arrays += [out_t]
        scratch += [pltpu.SemaphoreType.DMA((2,))]
    return pl.pallas_call(
        lambda *refs: kernel(n, sections, *refs),
        out_shape=outs,
        in_specs=[pl.BlockSpec(memory_space=pltpu.SMEM)] + [VMEM] * len(arrays),
        out_specs=[VMEM] * len(outs),
        scratch_shapes=scratch,
        compiler_params=pltpu.CompilerParams(collective_id=ident, has_side_effects=True, vmem_limit_bytes=LIMIT),
    )(cols, *arrays)


def shards(inputs, cotangent, weights, keep, columns):
    sections = lax.axis_size("section")
    section_id = lax.axis_index("section")
    n = lax.axis_size("zero")
    tokens, width = inputs.shape
    rows = width // BLK
    norm_factor = 1.0 / math.sqrt(tokens * n)
    own_keep = keep[0]
    own_rows = own_keep.shape[1]
    masked = weights[0] * own_keep[..., None].astype(BF)
    own = masked.reshape(3, own_rows, 2, BLK, BLK).transpose(0, 1, 3, 2, 4)
    own = own.reshape(3, own_rows, BLK, 2 * BLK)
    mats, start, cot = gather_all(own, inputs, cotangent, n, sections)
    cols = columns[0].reshape(-1)
    sec = jnp.stack([section_id, jnp.int32(sections)]).astype(jnp.int32)
    tall = (rows, BLK, tokens)
    wide = (NBC, BLK, tokens)
    (out,) = call(
        first_kernel, cols, sec, (start, mats), [(tall, BF)],
        [(tall, BF), (wide, F32), (wide, F32), (wide, BF)],
    )
    moved = lax.ppermute(out, "section", [(0, 1)])
    current = jnp.where(section_id == 0, start, moved)
    out, fa, fb, hid = call(
        middle_kernel, cols, sec, (current, cot, mats),
        [(tall, BF), (wide, BF), (wide, BF), (wide, BF)],
        [(tall, BF), (wide, F32), (wide, F32)],
    )
    is_upper = section_id == sections - 1
    sums_upper, gin_upper, out, upstream = reduce_all(
        upper_kernel, 1, n, sections, own_rows, cols, current, cot, mats, fa, fb, hid, out
    )
    gg, gu = call(
        last_kernel, cols, sec, (upstream, mats, fa, fb), [(wide, BF), (wide, BF)], [(wide, F32)]
    )
    sums_lower, gin_lower = reduce_all(
        lower_kernel, 2, n, sections, own_rows, cols, current, upstream, mats, gg, gu, hid
    )
    summed = jnp.where(is_upper, sums_upper, sums_lower)
    gin = jnp.where(is_upper, gin_upper, gin_lower)
    grad = summed.reshape(3, own_rows, BLK, 2, BLK).transpose(0, 1, 3, 2, 4)
    grad = grad.reshape(3, own_rows, 2, BLK * BLK)
    grad = grad * own_keep[..., None].astype(F32) * norm_factor
    return (out[None], gin[None], grad[None])


def solution(mesh):
    return jax.shard_map(
        shards,
        mesh=mesh,
        in_specs=(
            P(("groups", "zero"), None),
            P(("groups", "zero"), None),
            P("section", None, "zero", None, None),
            P("section", None, "zero", None),
            P("section", None, None, None),
        ),
        out_specs=(
            P("section", ("groups", "zero"), None),
            P("section", ("groups", "zero"), None),
            P("section", None, ("groups", "zero"), None, None),
        ),
        check_vma=False,
    )
```

```python
import math

import jax
import jax.numpy as jnp
from jax import lax
from jax.experimental import pallas as pl
from jax.experimental.pallas import tpu as pltpu
from jax.sharding import PartitionSpec as P

FF = 11008
BLK = 64
NBC = FF // BLK
BF = jnp.bfloat16
F32 = jnp.float32
epsilon = 1e-05

TN = (((0,), (0,)), ((), ()))
NT = (((1,), (1,)), ((), ()))


def dot(a, b, dims=(((1,), (0,)), ((), ()))):
    return lax.dot_general(a, b, dims, preferred_element_type=F32)


def total_rows(acc):
    return jnp.sum(acc, axis=0, keepdims=True)


def fold(value):
    return jnp.sum(value.reshape(-1, 8, value.shape[-1]), axis=0)


def looped(count, unroll, body):
    def step(i, carry):
        for k in range(unroll):
            body(i * unroll + k)
        return carry

    lax.fori_loop(0, count // unroll, step, 0)


def norm_scale(a_ref):
    rows, blk, tokens = a_ref.shape

    def add(i, acc):
        for k in range(4):
            v = a_ref[i * 4 + k].astype(F32)
            acc = acc + fold(v * v)
        return acc

    acc = lax.fori_loop(0, rows // 4, add, jnp.zeros((8, tokens), F32))
    return lax.rsqrt(total_rows(acc) / (rows * blk) + epsilon)


def column(cols, m, r, k, rows):
    return cols[(m * rows + r) * 2 + k]


def clear(*refs):
    def body(c):
        for ref in refs:
            ref[c] = jnp.zeros(ref.shape[1:], ref.dtype)

    looped(NBC, 4, body)


def spread(cols, m, rows, r, w, x, out):
    res = dot(w, x, TN)
    for k in range(2):
        c = column(cols, m, r, k, rows)
        out[c] += res[k * BLK : (k + 1) * BLK]


def pick(cols, m, rows, r, src):
    return [src[column(cols, m, r, k, rows)] for k in range(2)]


def forward_into(cols, a_ref, w_ref, out_ref, xn, pg, pu, hid, fa=None, fb=None):
    rows = a_ref.shape[0]
    recip = norm_scale(a_ref)

    def normed(r):
        xn[r] = (a_ref[r].astype(F32) * recip).astype(BF)

    looped(rows, 4, normed)
    clear(pg, pu)

    def up(r):
        x = xn[r]
        spread(cols, 0, rows, r, w_ref[0, r], x, pg)
        spread(cols, 1, rows, r, w_ref[1, r], x, pu)

    looped(rows, 4, up)

    def act(c):
        g = pg[c]
        u = pu[c]
        s = 1.0 / (1.0 + jnp.exp(-g))
        silu = g * s
        hid[c] = (silu * u).astype(BF)
        if fa is not None:
            fa[c] = (u * s * (1.0 + g * (1.0 - s))).astype(BF)
            fb[c] = silu.astype(BF)

    looped(NBC, 2, act)

    def down(r):
        o = dot(w_ref[2, r], jnp.concatenate(pick(cols, 2, rows, r, hid), axis=0))
        out_ref[r] = (a_ref[r].astype(F32) + o).astype(BF)

    looped(rows, 4, down)


def spread_back(cols, g_ref, w_ref, fa, fb, gh, gg, gu):
    rows = g_ref.shape[0]
    clear(gh)
    looped(rows, 4, lambda r: spread(cols, 2, rows, r, w_ref[2, r], g_ref[r], gh))

    def act(c):
        v = gh[c]
        gg[c] = (v * fa[c].astype(F32)).astype(BF)
        gu[c] = (v * fb[c].astype(F32)).astype(BF)

    looped(NBC, 2, act)


def back_sums(cols, a_ref, recip, w_ref, gg, gu, gn, first, last, acc):
    rows = a_ref.shape[0]

    def back(i, acc):
        for k in range(4):
            r = i * 4 + k
            right = pick(cols, 0, rows, r, gg) + pick(cols, 1, rows, r, gu)
            left = jnp.concatenate([w_ref[0, r], w_ref[1, r]], axis=1)
            v = dot(left, jnp.concatenate(right, axis=0))
            gn[r] = v
            acc = acc + fold(v * (a_ref[r].astype(F32) * recip))
        return acc

    return lax.fori_loop(first // 4, last // 4, back, acc)


def grad_rows(a_ref, g_ref, recip, gn, inner, r):
    q = a_ref[r].astype(F32) * recip
    return (g_ref[r].astype(F32) + recip * (gn[r] - q * inner)).astype(BF)


def first_kernel(cols, sec, a_ref, w_ref, out_ref, xn, pg, pu, hid):
    @pl.when(sec[0] < sec[1] - 1)
    def _():
        forward_into(cols, a_ref, w_ref, out_ref, xn, pg, pu, hid)


def middle_kernel(cols, sec, a_ref, g_ref, w_ref, out_ref, fa, fb, hid, xn, pg, pu):
    forward_into(cols, a_ref, w_ref, out_ref, xn, pg, pu, hid, fa, fb)

    @pl.when(sec[0] == sec[1] - 1)
    def _():
        spread_back(cols, g_ref, w_ref, fa, fb, pg, fa, fb)


def terms_at(cols, a_ref, g_ref, recip, gg, gu, hid, wg_ref, r):
    rows = a_ref.shape[0]
    x = (a_ref[r].astype(F32) * recip).astype(BF)
    right = pick(cols, 0, rows, r, gg) + pick(cols, 1, rows, r, gu)
    t = dot(x, jnp.concatenate(right, axis=0), NT).astype(BF)
    wg_ref[0, r] = t[:, : 2 * BLK]
    wg_ref[1, r] = t[:, 2 * BLK :]
    t = dot(g_ref[r], jnp.concatenate(pick(cols, 2, rows, r, hid), axis=0), NT)
    wg_ref[2, r] = t.astype(BF)


def last_kernel(cols, sec, g_ref, w_ref, fa, fb, gg, gu, gh):
    @pl.when(sec[0] < sec[1] - 1)
    def _():
        spread_back(cols, g_ref, w_ref, fa, fb, gh, gg, gu)


VMEM = pl.BlockSpec(memory_space=pltpu.VMEM)
ANY = pl.BlockSpec(memory_space=pl.ANY)
LIMIT = 58 * 2**20


def call(kernel, cols, sec, arrays, outs, scratch):
    return pl.pallas_call(
        kernel,
        out_shape=[jax.ShapeDtypeStruct(s, d) for s, d in outs],
        in_specs=[pl.BlockSpec(memory_space=pltpu.SMEM)] * 2 + [VMEM] * len(arrays),
        out_specs=[VMEM] * len(outs),
        scratch_shapes=[pltpu.VMEM(s, d) for s, d in scratch],
        compiler_params=pltpu.CompilerParams(vmem_limit_bytes=LIMIT),
    )(cols, sec, *arrays)


def places(n):
    half = n // 2
    me = lax.axis_index("zero")
    low = lax.rem(me, 2)
    mine = lax.div(me, 2)
    return me, me + 1 - 2 * low, half, low, mine


def remote(src, dst, send, recv, where):
    return pltpu.make_async_remote_copy(
        src_ref=src, dst_ref=dst, send_sem=send, recv_sem=recv,
        device_id=where, device_id_type=pl.DeviceIdType.MESH,
    )


def greet(targets):
    barrier = pltpu.get_barrier_semaphore()
    for t in targets:
        pl.semaphore_signal(barrier, inc=1, device_id=t, device_id_type=pl.DeviceIdType.MESH)
    pl.semaphore_wait(barrier, len(targets))


def gather_kernel(n, sections, own, x_ref, c_ref, out, xt_ref, ct_ref, local, zs, zr, ys, yr, go):
    me, partner, half, low, mine = places(n)
    sec = lax.axis_index("section")
    other = {"section": sections - 1 - sec}
    r_own = own.shape[1]

    def peer(d):
        return lax.rem(mine + d, half) * 2 + low

    def slot(m, who):
        return out.at[m, pl.ds(who * r_own, r_own)]

    greet([{"zero": peer(d)} for d in range(1, half)] + [{"zero": partner}, other])
    stays = [pltpu.make_async_copy(own.at[m], slot(m, me), local.at[m]) for m in range(3)]
    for c in stays:
        c.start()

    def transposed(p, carry):
        lanes = pl.ds(pl.multiple_of(p * 2 * BLK, 2 * BLK), 2 * BLK)
        for src, dst in ((x_ref, xt_ref), (c_ref, ct_ref)):
            t = src[:, lanes].T
            dst[2 * p] = t[:BLK]
            dst[2 * p + 1] = t[BLK:]
        return carry

    @pl.when(sec == sections - 1)
    def _():
        pl.semaphore_wait(go, 1)

    sent = []
    for m in range(3):
        for d in range(1, half):
            c = remote(own.at[m], slot(m, me), zs.at[m, d], zr.at[m, d], {"zero": peer(d)})
            c.start()
            sent.append(c)
        c = remote(own.at[m], slot(m, me), ys.at[m, 0], yr.at[m, 0], {"zero": partner})
        c.start()
        sent.append(c)
    pairs = x_ref.shape[1] // (2 * BLK)
    steps = 3 * (half - 1)
    for m in range(3):
        for d in range(1, half):
            at = m * (half - 1) + d - 1
            lax.fori_loop(at * pairs // steps, (at + 1) * pairs // steps, transposed, 0)
            who = lax.rem(mine + half - d, half) * 2 + low
            remote(own.at[m], slot(m, who), zs.at[m, d], zr.at[m, d], {"zero": partner}).wait_recv()
            c = remote(slot(m, who), slot(m, who), ys.at[m, d], yr.at[m, d], {"zero": partner})
            c.start()
            sent.append(c)

    @pl.when(sec == 0)
    def _():
        pl.semaphore_signal(go, inc=1, device_id=other, device_id_type=pl.DeviceIdType.MESH)

    for m in range(3):
        for d in range(half):
            who = lax.rem(mine + half - d, half) * 2 + 1 - low
            remote(own.at[m], slot(m, who), ys.at[m, d], yr.at[m, d], {"zero": partner}).wait_recv()

    for c in sent:
        c.wait_send()
    for c in stays:
        c.wait()


def flip(dst, rows_of, pairs):
    def body(p, carry):
        lanes = pl.ds(pl.multiple_of(p * 2 * BLK, 2 * BLK), 2 * BLK)
        dst[:, lanes] = jnp.concatenate([rows_of(2 * p), rows_of(2 * p + 1)], axis=0).T
        return carry

    lax.fori_loop(0, pairs, body, 0)


def hand_copy(gin_pass, sems, other):
    return remote(gin_pass, gin_pass, sems.at[0], sems.at[1], other)


def upper_kernel(n, sections, cols, a_ref, g_ref, w_ref, gg, gu, hid, out_t, sums, gin_ref, out_ref, gin_pass, *scratch):
    sec = lax.axis_index("section")
    other = {"section": sections - 1 - sec}
    hand = scratch[-1]
    pairs = a_ref.shape[0] // 2

    @pl.when(sec == sections - 1)
    def _():
        reduce_body(
            n, cols, a_ref, g_ref, w_ref, gg, gu, hid, sums, gin_ref, *scratch[:-1],
            upper=(out_t, out_ref, gin_pass, hand, other),
        )

    @pl.when(sec < sections - 1)
    def _():
        greet([other])
        flip(out_ref, lambda r: out_t[r], pairs)
        hand_copy(gin_pass, hand, other).wait_recv()


def lower_kernel(n, sections, cols, a_ref, g_ref, w_ref, gg, gu, hid, sums, gin_ref, *scratch):
    @pl.when(lax.axis_index("section") < sections - 1)
    def _():
        reduce_body(n, cols, a_ref, g_ref, w_ref, gg, gu, hid, sums, gin_ref, *scratch)


def reduce_body(
    n, cols, a_ref, g_ref, w_ref, gg, gu, hid, sums, gin_ref,
    terms, gn, near, mid, far, ys, yr, zs, zr, upper=None
):
    me, partner, half, low, mine = places(n)
    rows, blk, tokens = a_ref.shape
    r_own = sums.shape[1]
    peers = [{"zero": lax.rem(mine + d, half) * 2 + low} for d in range(1, half)]
    greet(peers + [{"zero": partner}] + ([upper[-1]] if upper else []))
    order = list(range(1, half)) + [0]
    todo = len(order)
    sent = []
    recip = norm_scale(a_ref)
    part = jnp.zeros((8, tokens), F32)

    def position(d):
        return lax.rem(mine + d, half) * 2

    def block_of(who):
        def body(r):
            terms_at(cols, a_ref, g_ref, recip, gg, gu, hid, terms, who * r_own + r)

        looped(r_own, 4, body)

    for i, d in enumerate(order):
        if i == 1 and upper:
            part = back_sums(cols, a_ref, recip, w_ref, gg, gu, gn, 0, rows, part)
            inner = total_rows(part) / (rows * blk)
            out_t, out_ref, gin_pass, hand, other = upper

            def finish(r):
                gin_pass[r] = grad_rows(a_ref, g_ref, recip, gn, inner, r)

            looped(rows, 4, finish)
            c = hand_copy(gin_pass, hand, other)
            c.start()
            sent.append(c)
        who = position(d) + 1 - low
        block_of(who)
        for m in range(3):
            src = terms.at[m, pl.ds(who * r_own, r_own)]
            c = remote(src, near.at[d, m], ys.at[d, m], yr.at[d, m], {"zero": partner})
            c.start()
            sent.append(c)

    for i, d in enumerate(order):
        block_of(position(d) + low)
        if not upper:
            first, last = (i * rows // todo, (i + 1) * rows // todo)
            part = back_sums(cols, a_ref, recip, w_ref, gg, gu, gn, first, last, part)
        for m in range(3):
            remote(near.at[d, m], near.at[d, m], ys.at[d, m], yr.at[d, m], {"zero": partner}).wait_recv()
            first = (position(d) + low) * r_own

            def add(r, carry):
                both = terms[m, first + r].astype(F32) + near[d, m, r].astype(F32)
                mid[d, m, r] = both.astype(BF)
                return carry

            lax.fori_loop(0, r_own, add, 0)
            if d:
                c = remote(
                    mid.at[d, m], far.at[d, m], zs.at[d, m], zr.at[d, m],
                    {"zero": position(d) + low},
                )
                c.start()
                sent.append(c)

    if upper:
        out_t, out_ref, gin_pass, hand, other = upper
        flip(out_ref, lambda r: out_t[r], rows // 2)
        flip(gin_ref, lambda r: gin_pass[r], rows // 2)
    else:
        inner = total_rows(part) / (rows * blk)
        flip(gin_ref, lambda r: grad_rows(a_ref, g_ref, recip, gn, inner, r), rows // 2)

    for m in range(3):
        for d in range(1, half):
            remote(mid.at[d, m], far.at[d, m], zs.at[d, m], zr.at[d, m], {"zero": partner}).wait_recv()

        def total(r, carry):
            value = mid[0, m, r].astype(F32)
            for d in range(1, half):
                value = value + far[d, m, r].astype(F32)
            sums[m, r] = value
            return carry

        lax.fori_loop(0, r_own, total, 0)
    for c in sent:
        c.wait_send()


def gather_all(own, x, c, n, sections):
    tokens, width = x.shape
    three, r_own, blk, two = own.shape
    half = n // 2
    tall = (width // BLK, BLK, tokens)
    sems = pltpu.SemaphoreType.DMA((3, half))
    return pl.pallas_call(
        lambda *refs: gather_kernel(n, sections, *refs),
        out_shape=[
            jax.ShapeDtypeStruct((three, n * r_own, blk, two), BF),
            jax.ShapeDtypeStruct(tall, BF),
            jax.ShapeDtypeStruct(tall, BF),
        ],
        in_specs=[ANY, VMEM, VMEM],
        out_specs=[ANY, VMEM, VMEM],
        scratch_shapes=[pltpu.SemaphoreType.DMA((3,)), sems, sems, sems, sems, pltpu.SemaphoreType.REGULAR],
        compiler_params=pltpu.CompilerParams(collective_id=0, has_side_effects=True, vmem_limit_bytes=LIMIT),
    )(own, x, c)


def reduce_all(kernel, ident, n, sections, own_rows, cols, a, g, mats, gg, gu, hid, out_t=None):
    three, rows, blk, two = mats.shape
    half = n // 2
    tokens = a.shape[2]
    flat = jax.ShapeDtypeStruct((tokens, rows * blk), BF)
    held = pltpu.VMEM((half, 3, own_rows, blk, two), BF)
    sems = pltpu.SemaphoreType.DMA((half, 3))
    outs = [jax.ShapeDtypeStruct((three, own_rows, blk, two), F32), flat]
    arrays = [a, g, mats, gg, gu, hid]
    scratch = [pltpu.VMEM(mats.shape, BF), pltpu.VMEM((rows, blk, tokens), F32)]
    scratch += [held, held, held, sems, sems, sems, sems]
    if out_t is not None:
        outs += [flat, jax.ShapeDtypeStruct(a.shape, BF)]
        arrays += [out_t]
        scratch += [pltpu.SemaphoreType.DMA((2,))]
    return pl.pallas_call(
        lambda *refs: kernel(n, sections, *refs),
        out_shape=outs,
        in_specs=[pl.BlockSpec(memory_space=pltpu.SMEM)] + [VMEM] * len(arrays),
        out_specs=[VMEM] * len(outs),
        scratch_shapes=scratch,
        compiler_params=pltpu.CompilerParams(collective_id=ident, has_side_effects=True, vmem_limit_bytes=LIMIT),
    )(cols, *arrays)


def shards(inputs, cotangent, weights, keep, columns):
    sections = lax.axis_size("section")
    section_id = lax.axis_index("section")
    n = lax.axis_size("zero")
    tokens, width = inputs.shape
    rows = width // BLK
    norm_factor = 1.0 / math.sqrt(tokens * n)
    own_keep = keep[0]
    own_rows = own_keep.shape[1]
    masked = weights[0] * own_keep[..., None].astype(BF)
    own = masked.reshape(3, own_rows, 2, BLK, BLK).transpose(0, 1, 3, 2, 4)
    own = own.reshape(3, own_rows, BLK, 2 * BLK)
    mats, start, cot = gather_all(own, inputs, cotangent, n, sections)
    cols = columns[0].reshape(-1)
    sec = jnp.stack([section_id, jnp.int32(sections)]).astype(jnp.int32)
    tall = (rows, BLK, tokens)
    wide = (NBC, BLK, tokens)
    (out,) = call(
        first_kernel, cols, sec, (start, mats), [(tall, BF)],
        [(tall, BF), (wide, F32), (wide, F32), (wide, BF)],
    )
    moved = lax.ppermute(out, "section", [(0, 1)])
    current = jnp.where(section_id == 0, start, moved)
    out, fa, fb, hid = call(
        middle_kernel, cols, sec, (current, cot, mats),
        [(tall, BF), (wide, BF), (wide, BF), (wide, BF)],
        [(tall, BF), (wide, F32), (wide, F32)],
    )
    is_upper = section_id == sections - 1
    sums_upper, gin_upper, out, upstream = reduce_all(
        upper_kernel, 1, n, sections, own_rows, cols, current, cot, mats, fa, fb, hid, out
    )
    gg, gu = call(
        last_kernel, cols, sec, (upstream, mats, fa, fb), [(wide, BF), (wide, BF)], [(wide, F32)]
    )
    sums_lower, gin_lower = reduce_all(
        lower_kernel, 2, n, sections, own_rows, cols, current, upstream, mats, gg, gu, hid
    )
    summed = jnp.where(is_upper, sums_upper, sums_lower)
    gin = jnp.where(is_upper, gin_upper, gin_lower)
    grad = summed.reshape(3, own_rows, BLK, 2, BLK).transpose(0, 1, 3, 2, 4)
    grad = grad.reshape(3, own_rows, 2, BLK * BLK)
    grad = grad * own_keep[..., None].astype(F32) * norm_factor
    return (out[None], gin[None], grad[None])


def solution(mesh):
    return jax.shard_map(
        shards,
        mesh=mesh,
        in_specs=(
            P(("groups", "zero"), None),
            P(("groups", "zero"), None),
            P("section", None, "zero", None, None),
            P("section", None, "zero", None),
            P("section", None, None, None),
        ),
        out_specs=(
            P("section", ("groups", "zero"), None),
            P("section", ("groups", "zero"), None),
            P("section", None, ("groups", "zero"), None, None),
        ),
        check_vma=False,
    )
```
